32 devices in a mesh: groups: 2 (over x), mp: 16 (over z, y, core).
Axes of the slice: x: 2, y: 2, z: 4, core: 2. Of those that a mesh axis runs over, the one named last changes fastest.
Arguments:
- stream: bfloat16 [256, 12288], P('groups', 'mp'), parts along dimension 0
- target_ids: int32 [256], P('groups'), parts along dimension 0, may hold values from 0 to 4095
- lengths: int32 [4], P('groups'), parts along dimension 0, may hold values from 1 to 64, as said below
- attn_gain: float32 [12288], replicated, may hold values from 0.1 to 1.9
- w_query: bfloat16 [12288, 2048], P(None, 'mp')
- w_key: bfloat16 [12288, 1024], P(None, 'mp')
- w_value: bfloat16 [12288, 1024], P(None, 'mp'), may hold values from -0.0546875 to 0.0546875
- w_out: bfloat16 [2048, 12288], P('mp'), may hold values from -0.125 to 0.125
- final_gain: float32 [12288], replicated, may hold values from 0.1 to 1.9
- lm_head: bfloat16 [12288, 4096], P(None, 'mp')
Outputs:
- layer_out: bfloat16 [256, 12288], P('groups', 'mp'), parts along dimension 0
- token_logprob: float32 [256], P('groups'), parts along dimension 0
The draws below stay inside these ranges and needn't reach their ends.
There are 2 independent parts, one for each index of `groups`. The reference program is written for one: setup_inputs(seed, part) draws one part's arguments, and reference() takes and returns one part's arrays. A program takes and returns all parts, laid end to end along the dimension named above; an argument that names none is the same for every part. Nothing has to cross between parts.
Inputs may be any that keep to these rules, and one draw needn't show every extreme that they name: `lengths`: one slot has length 64.
All inputs are finite; a program needn't handle non-finite values.
Results may differ from the reference program's by a relative error of at most 0.0068.
Values may be sent and summed in bfloat16 or wider, within the bound.
A program may use at most 64 MiB of HBM per device.

```python
import jax
import jax.numpy as jnp
from jax import lax

D = 12288
KVH = 8
HD = 128
TOKENS = 128
SEQS = 2
HEADS = 16
VOCAB = 4096
LEN = 64


def draw_stream(key, part):
    key = jax.random.fold_in(key, 9)
    first, second, third = jax.random.split(key, 3)
    ramp = jnp.arange(D, dtype=jnp.float32) / max(D - 1, 1)
    base = jnp.clip(jax.random.normal(first, (TOKENS, D), jnp.float32), -6.0, 6.0)
    column = jnp.power(3.0, ramp) * jnp.exp(jax.random.uniform(second, (D,), jnp.float32, -0.35, 0.35)) / 1.7
    row = jnp.exp(jax.random.uniform(third, (TOKENS, 1), jnp.float32, -0.69, 0.69))
    return (base * column[None, :] * row).astype(jnp.bfloat16)


def draw_lengths(key, part):
    key = jax.random.fold_in(key, 5)
    first, second = jax.random.split(key)
    base = jax.random.randint(first, (SEQS,), 1, LEN + 1)
    full_slot = jax.random.randint(second, (), 0, SEQS)
    return jnp.where(jnp.arange(SEQS) == full_slot, LEN, base).astype(jnp.int32)


def draw_w_query(key, part):
    key = jax.random.fold_in(key, 21)
    result = jax.random.normal(key, (D, HEADS * HD), jnp.float32) * D ** (-0.5)
    return result.astype(jnp.bfloat16)


def draw_w_key(key, part):
    key = jax.random.fold_in(key, 33)
    result = jax.random.normal(key, (D, KVH * HD), jnp.float32) * D ** (-0.5)
    return result.astype(jnp.bfloat16)


def draw_lm_head(key, part):
    key = jax.random.fold_in(key, 47)
    factor = 3.0
    result = jax.random.normal(key, (D, VOCAB), jnp.float32) * (factor / D ** 0.5)
    return result.astype(jnp.bfloat16)


def touch_ends(array, rng, low, largest):
    shape = array.shape
    place = [jax.random.randint(jax.random.fold_in(rng, axis), (), 0, shape[axis]) for axis in range(len(shape))]
    array = array.at[tuple(place)].set(low)
    longest = shape.index(max(shape))
    place[longest] = (place[longest] + 1) % shape[longest]
    return array.at[tuple(place)].set(largest)


def shard_levels(rng, extent, shards, smallest, high):
    level = 1.0
    for dim, blocks in shards:
        heights = jax.random.uniform(jax.random.fold_in(jax.random.fold_in(rng, 6), dim), (blocks,), jnp.float32, smallest / len(shards), high / len(shards))
        level = level * jnp.repeat(jnp.exp(heights), extent[dim] // blocks).reshape((-1,) + (1,) * (len(extent) - 1 - dim))
    return level


def bell_draw(key, shape, scale, limit, cuts=(), kind=jnp.bfloat16):
    array = scale * jax.random.normal(key, shape, jnp.float32)
    if cuts:
        array = array * shard_levels(key, shape, cuts, -0.22, 0.18)
    return jnp.clip(array, -limit, limit).astype(kind)


def setup_inputs(seed: int = 0, part: int = 0) -> dict:
    arg_keys = jax.random.split(jax.random.key(seed), 11)
    own_keys = jax.random.split(jax.random.fold_in(arg_keys[10], part), 11)
    return {
        "stream": draw_stream(jax.random.fold_in(jax.random.fold_in(arg_keys[10], part), 71), part),
        "target_ids": touch_ends(jax.random.randint(own_keys[1], (TOKENS,), 0, VOCAB), jax.random.fold_in(own_keys[1], 1), 0, VOCAB - 1).astype(jnp.int32),
        "lengths": draw_lengths(jax.random.fold_in(jax.random.fold_in(arg_keys[10], part), 71), part),
        "attn_gain": jnp.clip(1.0 + 0.18 * jax.random.normal(arg_keys[3], (D,), jnp.float32), 0.1, 1.9),
        "w_query": draw_w_query(jax.random.fold_in(arg_keys[10], 71), part),
        "w_key": draw_w_key(jax.random.fold_in(arg_keys[10], 71), part),
        "w_value": bell_draw(arg_keys[6], (D, KVH * HD), D ** -0.5, 0.0546875, ((1, 16),)),
        "w_out": bell_draw(arg_keys[7], (HEADS * HD, D), (HEADS * HD) ** -0.5, 0.125, ((0, 16),)),
        "final_gain": jnp.clip(1.0 + 0.18 * jax.random.normal(arg_keys[8], (D,), jnp.float32), 0.1, 1.9),
        "lm_head": draw_lm_head(jax.random.fold_in(arg_keys[10], 71), part),
    }


def norm_rows(values, gain):
    wide = values.astype(jnp.float32)
    scale = lax.rsqrt(lax.optimization_barrier(jnp.mean(wide * wide, axis=-1, keepdims=True)) + 1e-05)
    return wide * scale * gain

def rotate(values, positions, first_col):
    rows, cols = values.shape
    pairs = jnp.arange(cols // 2, dtype=jnp.int32)
    within = (first_col + 2 * pairs) % HD
    freq = jnp.power(jnp.float32(1000000.0), -within.astype(jnp.float32) / HD)
    angle = positions.astype(jnp.float32)[:, None] * freq[None, :]
    cosine = jnp.cos(angle)
    sine = jnp.sin(angle)
    paired = values.reshape(rows, cols // 2, 2)
    first = paired[:, :, 0]
    second = paired[:, :, 1]
    turned = jnp.stack([first * cosine - second * sine, first * sine + second * cosine], axis=-1)
    return turned.reshape(rows, cols)

def reference(stream, target_ids, lengths, attn_gain, w_query, w_key, w_value, w_out, final_gain, lm_head):
    normed = norm_rows(stream, attn_gain).astype(jnp.bfloat16)
    rows = jnp.arange(TOKENS, dtype=jnp.int32)
    positions = rows % LEN
    slots = rows // LEN
    query = rotate(jnp.dot(normed, w_query, preferred_element_type=jnp.float32), positions, 0).astype(jnp.bfloat16)
    keys = rotate(jnp.dot(normed, w_key, preferred_element_type=jnp.float32), positions, 0).astype(jnp.bfloat16)
    values = jnp.dot(normed, w_value, preferred_element_type=jnp.float32).astype(jnp.bfloat16)
    slot_len = lax.optimization_barrier(jnp.sum(jnp.where(slots[:, None] == jnp.arange(SEQS, dtype=jnp.int32)[None, :], lengths[None, :], 0), axis=1))
    visible = (slots[None, :] == slots[:, None]) & (positions[None, :] <= positions[:, None]) & (positions[None, :] < slot_len[None, :])

    def one_head(head):
        q_head = lax.dynamic_slice_in_dim(query, (head * HD).astype(jnp.int32), HD, 1)
        kv_start = (head % KVH * HD).astype(jnp.int32)
        k_head = lax.dynamic_slice_in_dim(keys, kv_start, HD, 1)
        v_head = lax.dynamic_slice_in_dim(values, kv_start, HD, 1)
        scores = jnp.dot(q_head, k_head.T, preferred_element_type=jnp.float32) / jnp.sqrt(jnp.float32(HD))
        scores = jnp.where(visible, scores, jnp.float32(-1e+30))
        top = lax.optimization_barrier(jnp.max(scores, axis=1, keepdims=True))
        weights = jnp.exp(scores - top)
        probs = (weights / lax.optimization_barrier(jnp.sum(weights, axis=1, keepdims=True))).astype(jnp.bfloat16)
        return jnp.dot(probs, v_head, preferred_element_type=jnp.float32).astype(jnp.bfloat16)
    heads = lax.map(one_head, jnp.arange(HEADS, dtype=jnp.int32))
    attn = jnp.transpose(heads, (1, 0, 2)).reshape(TOKENS, HEADS * HD)
    summed = jnp.dot(attn, w_out, preferred_element_type=jnp.float32)
    layer_out = (stream.astype(jnp.float32) + summed).astype(jnp.bfloat16)
    final = norm_rows(layer_out, final_gain).astype(jnp.bfloat16)
    logits = jnp.dot(final, lm_head, preferred_element_type=jnp.float32)
    top = lax.optimization_barrier(jnp.max(logits, axis=1))
    total = lax.optimization_barrier(jnp.sum(jnp.exp(logits - top[:, None]), axis=1))
    picked = jnp.take_along_axis(logits, target_ids[:, None].astype(jnp.int32), axis=1)[:, 0]
    token_logprob = picked - top - jnp.log(total)
    return (layer_out, token_logprob)
```

```python
import functools

import jax
import jax.numpy as jnp
import numpy as np
from jax import lax
from jax.experimental import pallas as pl
from jax.experimental.pallas import tpu as pltpu
from jax.sharding import PartitionSpec as P

KVH = 8
HD = 128
SEQS = 2
B, C = 2, 2
BF16, F32 = jnp.bfloat16, jnp.float32


def rope_tables(tokens):
    positions = (np.arange(tokens) % (tokens // SEQS)).astype(np.float32)
    within = 2 * (np.arange(HD) // 2)
    freq = np.power(np.float32(1000000.0), -within.astype(np.float32) / np.float32(HD))
    angle = (positions[:, None] * freq[None, :].astype(np.float32)).astype(np.float32)
    sine = np.sin(angle.astype(np.float64))
    sine = np.where(np.arange(HD)[None, :] % 2 == 0, -sine, sine)
    return np.cos(angle.astype(np.float64)).astype(np.float32), sine.astype(np.float32)


def rope(values, cosine, sine):
    even = lax.broadcasted_iota(jnp.int32, values.shape, 1) % 2 == 0
    swapped = jnp.where(even, pltpu.roll(values, HD - 1, 1), pltpu.roll(values, 1, 1))
    return values * cosine + swapped * sine


def kernel(
    n, depth,
    x_ref, ids_ref, len_ref, gain1_ref, gain2_ref, cos_ref, sin_ref,
    wq_hbm, wk_hbm, wv_hbm, wo_hbm, lm_hbm,
    out_ref, logp_ref,
    wq, wk, wv, wo, lm, X1, X2, acc_q, acc_k, acc_v, ssq, acc_l,
    kvs, kvr, attn, cs, cr, ys, yr, us, ur, ds, dr, tot, st,
    wsem, wosem, ag_s1, ag_r1, ag_s2, ag_r2, kv_s, kv_r,
    cs_s, cs_r, ys_s, ys_r, us_s, us_r, ds_s, ds_r, st_s, st_r,
):
    A = n // (B * C)
    me = lax.axis_index("mp")
    c = lax.rem(me, C)
    y = lax.rem(lax.div(me, C), B)
    z = lax.div(me, B * C)
    tokens, width = x_ref.shape
    kv_cols = wk.shape[2]
    pieces = HD // kv_cols
    users = n // KVH

    def idx(zz, yy, cc):
        return (zz * B + yy) * C + cc

    core, side = idx(z, y, 1 - c), idx(z, 1 - y, c)
    above, below = idx(z + 1, y, c), idx(z - 1, y, c)

    def rc(src, dst, ssem, rsem, dev):
        return pltpu.make_async_remote_copy(
            src_ref=src, dst_ref=dst, send_sem=ssem, recv_sem=rsem,
            device_id={"mp": dev}, device_id_type=pl.DeviceIdType.MESH,
        )

    loads = [
        pltpu.make_async_copy(src, dst, wsem.at[i])
        for i, (src, dst) in enumerate(((wq_hbm, wq), (wk_hbm, wk), (wv_hbm, wv), (lm_hbm, lm)))
    ]

    def wo_load(j):
        src = wo_hbm.at[j] if len(wo_hbm.shape) == 3 else wo_hbm.at[:, j * width:(j + 1) * width]
        return pltpu.make_async_copy(src, wo.at[j], wosem.at[j])

    barrier = pltpu.get_barrier_semaphore()

    def greet(i, carry):
        pl.semaphore_signal(
            barrier, inc=1, device_id={"mp": lax.rem(me + i, n)}, device_id_type=pl.DeviceIdType.MESH
        )
        return carry

    lax.fori_loop(1, n, greet, 0)
    for load in loads[:3]:
        load.start()
    X1[me] = x_ref[...]
    acc_q[...] = jnp.zeros_like(acc_q)
    acc_k[...] = jnp.zeros_like(acc_k)
    acc_v[...] = jnp.zeros_like(acc_v)
    acc_l[...] = jnp.zeros_like(acc_l)
    ssq[...] = jnp.zeros_like(ssq)
    pl.semaphore_wait(barrier, n - 1)

    def gather(X, ss, rs, consume, prepare):
        def send(slot, kind, k, dev):
            return rc(X.at[slot], X.at[slot], ss.at[kind, k], rs.at[slot], dev)

        def got(slot):
            rc(X.at[slot], X.at[slot], ss.at[0, 0], rs.at[slot], core).wait_recv()

        @pl.when(z < A - 1)
        def _():
            send(me, 0, z, above).start()

        @pl.when(z > 0)
        def _():
            send(me, 1, z, below).start()

        send(me, 2, z, side).start()
        send(me, 3, z * B + y, core).start()
        prepare()
        consume(me)

        def valid(k, g, zz):
            return (k >= 0) & (k < A) & (zz >= 0) & (zz < A) & ((k > 0) | (g == 0))

        def step(s, carry):
            def line(g, carry):
                zz = z + (2 * g - 1) * s

                @pl.when(valid(s, g, zz))
                def _():
                    slot = idx(zz, y, c)
                    got(slot)

                    @pl.when((g == 0) & (z < A - 1))
                    def _():
                        send(slot, 0, zz, above).start()

                    @pl.when((g == 1) & (z > 0))
                    def _():
                        send(slot, 1, zz, below).start()

                    send(slot, 2, zz, side).start()
                    send(slot, 3, zz * B + y, core).start()

                return carry

            lax.fori_loop(0, 2, line, 0)

            def line_use(g, carry):
                zz = z + (2 * g - 1) * s

                @pl.when(valid(s, g, zz))
                def _():
                    consume(idx(zz, y, c))

                return carry

            lax.fori_loop(0, 2, line_use, 0)

            def across(g, carry):
                zz = z + (2 * g - 1) * (s - 1)

                @pl.when(valid(s - 1, g, zz))
                def _():
                    slot = idx(zz, 1 - y, c)
                    got(slot)
                    send(slot, 3, zz * B + 1 - y, core).start()
                    consume(slot)
                    slot2 = idx(zz, y, 1 - c)
                    got(slot2)
                    consume(slot2)

                return carry

            lax.fori_loop(0, 2, across, 0)

            def last(g, carry):
                zz = z + (2 * g - 1) * (s - 2)

                @pl.when(valid(s - 2, g, zz))
                def _():
                    slot = idx(zz, 1 - y, 1 - c)
                    got(slot)
                    consume(slot)

                return carry

            lax.fori_loop(0, 2, last, 0)
            return carry

        lax.fori_loop(1, A + 2, step, 0)

        def drain(zz, carry):
            slot = idx(zz, y, c)

            @pl.when((zz <= z) & (z < A - 1))
            def _():
                send(slot, 0, zz, above).wait_send()

            @pl.when((zz >= z) & (z > 0))
            def _():
                send(slot, 1, zz, below).wait_send()

            send(slot, 2, zz, side).wait_send()
            send(slot, 3, zz * B + y, core).wait_send()
            other = idx(zz, 1 - y, c)
            send(other, 3, zz * B + 1 - y, core).wait_send()
            return carry

        return lambda: lax.fori_loop(0, A, drain, 0)

    def project(slot):
        wide = X1[slot].astype(F32)
        ssq[...] += jnp.sum(wide * wide, axis=1, keepdims=True)
        piece = (wide * gain1_ref[slot]).astype(BF16)
        acc_q[...] += jnp.dot(piece, wq[slot], preferred_element_type=F32)
        acc_k[...] += jnp.dot(piece, wk[slot], preferred_element_type=F32)
        acc_v[...] += jnp.dot(piece, wv[slot], preferred_element_type=F32)

    def ready():
        for load in loads[:3]:
            load.wait()
        for j in range(n):
            wo_load(j).start()
        loads[3].start()

    drain1 = gather(X1, ag_s1, ag_r1, project, ready)

    scale = lax.rsqrt(ssq[...] / depth + 1e-05)
    kvs[0] = acc_k[...] * scale
    kvs[1] = acc_v[...] * scale
    piece_id, head_of = lax.rem(me, pieces), lax.div(me, pieces)

    def kv_send(i):
        return rc(kvs, kvr.at[piece_id], kv_s.at[i], kv_r.at[piece_id], head_of + KVH * i)

    for i in range(users):
        @pl.when(head_of + KVH * i != me)
        def _():
            kv_send(i).start()

        @pl.when(head_of + KVH * i == me)
        def _():
            kvr[piece_id] = kvs[...]

    cosine, sine = cos_ref[...], sin_ref[...]
    query = rope(acc_q[...] * scale, cosine, sine).astype(BF16)
    source = lax.rem(me, KVH) * pieces
    for i in range(pieces):
        @pl.when(source + i != me)
        def _():
            rc(kvs, kvr.at[i], kv_s.at[0], kv_r.at[i], core).wait_recv()

    key = jnp.concatenate([kvr[i, 0] for i in range(pieces)], axis=1)
    key = rope(key, cosine, sine).astype(BF16)
    value = jnp.concatenate([kvr[i, 1] for i in range(pieces)], axis=1).astype(BF16)
    seq_len = tokens // SEQS
    row = lax.broadcasted_iota(jnp.int32, (tokens, tokens), 0)
    col = lax.broadcasted_iota(jnp.int32, (tokens, tokens), 1)
    limit = jnp.full((tokens, tokens), len_ref[0], jnp.int32)
    for i in range(1, SEQS):
        limit = jnp.where(col >= i * seq_len, len_ref[i], limit)
    visible = (row // seq_len == col // seq_len) & (col <= row) & (col % seq_len < limit)
    scores = lax.dot_general(query, key, (((1,), (1,)), ((), ())), preferred_element_type=F32)
    scores = jnp.where(visible, scores / np.float32(np.sqrt(HD)), jnp.float32(-1e30))
    weights = jnp.exp(scores - jnp.max(scores, axis=1, keepdims=True))
    probs = (weights / jnp.sum(weights, axis=1, keepdims=True)).astype(BF16)
    attn[...] = jnp.dot(probs, value, preferred_element_type=F32).astype(BF16)
    for j in range(n):
        wo_load(j).wait()

    def partial(slot):
        return jnp.dot(attn[...], wo[slot], preferred_element_type=F32)

    def far_first(body):
        def step(i, carry):
            s = A - 1 - lax.div(i, 2)
            zz = z + (1 - 2 * lax.rem(i, 2)) * s

            @pl.when((zz >= 0) & (zz < A) & ((s > 0) | (lax.rem(i, 2) == 0)))
            def _():
                body(zz)

            return carry

        lax.fori_loop(0, 2 * A, step, 0)

    def core_copy(yy, zz):
        return rc(cs.at[yy, zz], cr.at[yy, zz], cs_s.at[yy, zz], cs_r.at[yy, zz], core)

    def to_core(yy):
        def body(zz):
            cs[yy, zz] = partial(idx(zz, yy, 1 - c)).astype(BF16)
            core_copy(yy, zz).start()

        return body

    def side_copy(zz):
        return rc(ys.at[zz], yr.at[zz], ys_s.at[zz], ys_r.at[zz], side)

    def to_side(zz):
        total = partial(idx(zz, 1 - y, c))
        core_copy(1 - y, zz).wait_recv()
        ys[zz] = (total + cr[1 - y, zz].astype(F32)).astype(BF16)
        side_copy(zz).start()

    def up_copy(zz):
        return rc(us.at[zz], ur.at[zz], us_s.at[zz], us_r.at[zz], above)

    def down_copy(zz):
        return rc(ds.at[zz], dr.at[zz], ds_s.at[zz], ds_r.at[zz], below)

    def both(zz):
        to_core(1 - y)(zz)

    far_first(both)
    far_first(to_side)
    far_first(lambda zz: to_core(y)(zz))

    def along(zz):
        total = partial(idx(zz, y, c))
        core_copy(y, zz).wait_recv()
        total += cr[y, zz].astype(F32)
        side_copy(zz).wait_recv()
        acc = total + yr[zz].astype(F32)

        @pl.when(zz > z)
        def _():
            @pl.when(z > 0)
            def _():
                up_copy(zz).wait_recv()
                us[zz] = (acc + ur[zz].astype(F32)).astype(BF16)

            @pl.when(z == 0)
            def _():
                us[zz] = acc.astype(BF16)

            up_copy(zz).start()

        @pl.when(zz < z)
        def _():
            @pl.when(z < A - 1)
            def _():
                down_copy(zz).wait_recv()
                ds[zz] = (acc + dr[zz].astype(F32)).astype(BF16)

            @pl.when(z == A - 1)
            def _():
                ds[zz] = acc.astype(BF16)

            down_copy(zz).start()

        @pl.when(zz == z)
        def _():
            tot[...] = acc

            @pl.when(z > 0)
            def _():
                up_copy(zz).wait_recv()
                tot[...] += ur[zz].astype(F32)

            @pl.when(z < A - 1)
            def _():
                down_copy(zz).wait_recv()
                tot[...] += dr[zz].astype(F32)

    far_first(along)
    layer = (x_ref[...].astype(F32) + tot[...]).astype(BF16)
    out_ref[...] = layer
    X2[me] = layer
    ssq[...] = jnp.zeros_like(ssq)

    def score(slot):
        wide = X2[slot].astype(F32)
        ssq[...] += jnp.sum(wide * wide, axis=1, keepdims=True)
        piece = (wide * gain2_ref[slot]).astype(BF16)
        acc_l[...] += jnp.dot(piece, lm[slot], preferred_element_type=F32)

    drain2 = gather(X2, ag_s2, ag_r2, score, loads[3].wait)

    logits = jnp.transpose(acc_l[...] * lax.rsqrt(ssq[...] / depth + 1e-05))
    vocab = logits.shape[0]
    word = lax.broadcasted_iota(jnp.int32, logits.shape, 0) + me * vocab
    picked = jnp.sum(jnp.where(word == ids_ref[...], logits, 0.0), axis=0, keepdims=True)
    top = jnp.max(logits, axis=0, keepdims=True)
    total = jnp.sum(jnp.exp(logits - top), axis=0, keepdims=True)
    st[me] = jnp.concatenate([top, total, picked, jnp.zeros((5, tokens), F32)], axis=0)

    def st_copy(slot, i, dev):
        return rc(st.at[slot], st.at[slot], st_s.at[i], st_r.at[slot], dev)

    def st_send(i, carry):
        st_copy(me, i, lax.rem(me + i, n)).start()
        return carry

    lax.fori_loop(1, n, st_send, 0)

    drain1()
    drain2()
    for i in range(users):
        @pl.when(head_of + KVH * i != me)
        def _():
            kv_send(i).wait_send()

    def rs_drain(zz, carry):
        core_copy(0, zz).wait_send()
        core_copy(1, zz).wait_send()
        side_copy(zz).wait_send()

        @pl.when(zz > z)
        def _():
            up_copy(zz).wait_send()

        @pl.when(zz < z)
        def _():
            down_copy(zz).wait_send()

        return carry

    lax.fori_loop(0, A, rs_drain, 0)

    def st_got(i, carry):
        slot = lax.rem(me + i, n)
        st_copy(slot, i, core).wait_recv()
        st_copy(me, i, slot).wait_send()
        return carry

    lax.fori_loop(1, n, st_got, 0)
    parts = st[...]
    tops, totals, hits = parts[:, 0, :], parts[:, 1, :], parts[:, 2, :]
    peak = jnp.max(tops, axis=0, keepdims=True)
    whole = jnp.sum(totals * jnp.exp(tops - peak), axis=0, keepdims=True)
    logp_ref[...] = jnp.sum(hits, axis=0, keepdims=True) - peak - jnp.log(whole)


def body(
    stream, target_ids, lengths, attn_gain, w_query, w_key, w_value, w_out, final_gain, lm_head
):
    tokens, width = stream.shape
    depth = w_query.shape[0]
    n = depth // width
    A = n // (B * C)
    kv_cols, vocab = w_key.shape[1], lm_head.shape[1]
    users, pieces = n // KVH, HD // kv_cols
    cosine, sine = rope_tables(tokens)
    if width % 128:
        w_out = w_out.reshape(HD, n, width).transpose(1, 0, 2)
    vmem = pl.BlockSpec(memory_space=pltpu.VMEM)
    smem = pl.BlockSpec(memory_space=pltpu.SMEM)
    hbm = pl.BlockSpec(memory_space=pl.ANY)
    block = (tokens, width)
    dma = pltpu.SemaphoreType.DMA
    V = pltpu.VMEM
    layer_out, logp = pl.pallas_call(
        functools.partial(kernel, n, depth),
        out_shape=(
            jax.ShapeDtypeStruct(block, BF16),
            jax.ShapeDtypeStruct((1, tokens), F32),
        ),
        in_specs=[vmem, vmem, smem] + [vmem] * 4 + [hbm] * 5,
        out_specs=(vmem, vmem),
        scratch_shapes=[
            V((n, width, HD), BF16), V((n, width, kv_cols), BF16), V((n, width, kv_cols), BF16),
            V((n, HD, width), BF16), V((n, width, vocab), BF16),
            V((n,) + block, BF16), V((n,) + block, BF16),
            V((tokens, HD), F32), V((tokens, kv_cols), F32), V((tokens, kv_cols), F32),
            V((tokens, 1), F32), V((tokens, vocab), F32),
            V((2, tokens, kv_cols), F32), V((pieces, 2, tokens, kv_cols), F32),
            V((tokens, HD), BF16),
            V((2, A) + block, BF16), V((2, A) + block, BF16),
            V((A,) + block, BF16), V((A,) + block, BF16),
            V((A,) + block, BF16), V((A,) + block, BF16),
            V((A,) + block, BF16), V((A,) + block, BF16),
            V(block, F32), V((n, 8, tokens), F32),
            dma((4,)), dma((n,)),
            dma((4, B * A)), dma((n,)), dma((4, B * A)), dma((n,)),
            dma((users,)), dma((pieces,)),
            dma((2, A)), dma((2, A)), dma((A,)), dma((A,)),
            dma((A,)), dma((A,)), dma((A,)), dma((A,)),
            dma((n,)), dma((n,)),
        ],
        compiler_params=pltpu.CompilerParams(
            collective_id=0, has_side_effects=True, vmem_limit_bytes=56 * 1024 * 1024
        ),
        cost_estimate=pl.CostEstimate(
            flops=2 * tokens * depth * (2 * HD + 2 * kv_cols + vocab),
            bytes_accessed=2 * depth * (2 * HD + 2 * kv_cols + vocab),
            transcendentals=0,
        ),
    )(
        stream, target_ids.reshape(1, tokens), lengths,
        attn_gain.reshape(n, 1, width), final_gain.reshape(n, 1, width),
        jnp.asarray(cosine), jnp.asarray(sine),
        w_query.reshape(n, width, HD), w_key.reshape(n, width, kv_cols),
        w_value.reshape(n, width, kv_cols), w_out, lm_head.reshape(n, width, vocab),
    )
    return layer_out, logp.reshape(tokens)


def solution(mesh):
    return jax.shard_map(
        body,
        mesh=mesh,
        in_specs=(
            P("groups", "mp"),
            P("groups"),
            P("groups"),
            P(),
            P(None, "mp"),
            P(None, "mp"),
            P(None, "mp"),
            P("mp", None),
            P(),
            P(None, "mp"),
        ),
        out_specs=(P("groups", "mp"), P("groups")),
        check_vma=False,
    )
```

```python
import functools

import jax
import jax.numpy as jnp
import numpy as np
from jax import lax
from jax.experimental import pallas as pl
from jax.experimental.pallas import tpu as pltpu
from jax.sharding import PartitionSpec as P

KVH = 8
HD = 128
SEQS = 2
B, C = 2, 2
BF16, F32 = jnp.bfloat16, jnp.float32


def rope_tables(tokens):
    positions = (np.arange(tokens) % (tokens // SEQS)).astype(np.float32)
    within = 2 * (np.arange(HD) // 2)
    freq = np.power(np.float32(1000000.0), -within.astype(np.float32) / np.float32(HD))
    angle = (positions[:, None] * freq[None, :].astype(np.float32)).astype(np.float32)
    sine = np.sin(angle.astype(np.float64))
    sine = np.where(np.arange(HD)[None, :] % 2 == 0, -sine, sine)
    return np.cos(angle.astype(np.float64)).astype(np.float32), sine.astype(np.float32)


def rope(values, cosine, sine):
    even = lax.broadcasted_iota(jnp.int32, values.shape, 1) % 2 == 0
    swapped = jnp.where(even, pltpu.roll(values, HD - 1, 1), pltpu.roll(values, 1, 1))
    return values * cosine + swapped * sine


def kernel(
    n, depth,
    x_ref, ids_ref, len_ref, gain1_ref, gain2_ref, cos_ref, sin_ref,
    wq_hbm, wk_hbm, wv_hbm, wo_hbm, lm_hbm,
    out_ref, logp_ref,
    wq, wkv, wo, lm, X1, X2, acc_q, acc_kv, ssq, acc_l,
    kvs, kvr, attn, cs, cr, ys, yr, us, ur, ds, dr, tot, st,
    wsem, wkvsem, wosem, ag_s1, ag_r1, ag_s2, ag_r2, kv_s, kv_r,
    cs_s, cs_r, ys_s, ys_r, us_s, us_r, ds_s, ds_r, st_s, st_r,
):
    A = n // (B * C)
    me = lax.axis_index("mp")
    c = lax.rem(me, C)
    y = lax.rem(lax.div(me, C), B)
    z = lax.div(me, B * C)
    tokens, width = x_ref.shape
    kv_cols = wkv.shape[1] // 2
    pieces = HD // kv_cols
    users = n // KVH

    def idx(zz, yy, cc):
        return (zz * B + yy) * C + cc

    core, side = idx(z, y, 1 - c), idx(z, 1 - y, c)
    above, below = idx(z + 1, y, c), idx(z - 1, y, c)

    def rc(src, dst, ssem, rsem, dev):
        return pltpu.make_async_remote_copy(
            src_ref=src, dst_ref=dst, send_sem=ssem, recv_sem=rsem,
            device_id={"mp": dev}, device_id_type=pl.DeviceIdType.MESH,
        )

    def columns(ref, j):
        return ref.at[j] if len(ref.shape) == 3 else ref.at[:, j * width:(j + 1) * width]

    q_load = pltpu.make_async_copy(wq_hbm, wq, wsem.at[0])
    lm_load = pltpu.make_async_copy(lm_hbm, lm, wsem.at[1])

    def kv_load(i, j):
        return pltpu.make_async_copy(
            columns((wk_hbm, wv_hbm)[i], j),
            wkv.at[j, i * kv_cols:(i + 1) * kv_cols],
            wkvsem.at[i, j],
        )

    def wo_load(j):
        return pltpu.make_async_copy(columns(wo_hbm, j), wo.at[j], wosem.at[j])

    barrier = pltpu.get_barrier_semaphore()

    def greet(i, carry):
        pl.semaphore_signal(
            barrier, inc=1, device_id={"mp": lax.rem(me + i, n)}, device_id_type=pl.DeviceIdType.MESH
        )
        return carry

    lax.fori_loop(1, n, greet, 0)
    q_load.start()
    for j in range(n):
        kv_load(0, j).start()
        kv_load(1, j).start()
    X1[me] = x_ref[...]
    acc_q[...] = jnp.zeros_like(acc_q)
    acc_kv[...] = jnp.zeros_like(acc_kv)
    acc_l[...] = jnp.zeros_like(acc_l)
    ssq[...] = jnp.zeros_like(ssq)
    pl.semaphore_wait(barrier, n - 1)

    def gather(X, ss, rs, consume, prepare):
        def send(slot, kind, k, dev):
            return rc(X.at[slot], X.at[slot], ss.at[kind, k], rs.at[slot], dev)

        def got(slot):
            rc(X.at[slot], X.at[slot], ss.at[0, 0], rs.at[slot], core).wait_recv()

        @pl.when(z < A - 1)
        def _():
            send(me, 0, z, above).start()

        @pl.when(z > 0)
        def _():
            send(me, 1, z, below).start()

        send(me, 2, z, side).start()
        send(me, 3, z * B + y, core).start()
        prepare()
        consume(me)

        def valid(k, g, zz):
            return (k >= 0) & (k < A) & (zz >= 0) & (zz < A) & ((k > 0) | (g == 0))

        def step(s, carry):
            def line(g, carry):
                zz = z + (2 * g - 1) * s

                @pl.when(valid(s, g, zz))
                def _():
                    slot = idx(zz, y, c)
                    got(slot)

                    @pl.when((g == 0) & (z < A - 1))
                    def _():
                        send(slot, 0, zz, above).start()

                    @pl.when((g == 1) & (z > 0))
                    def _():
                        send(slot, 1, zz, below).start()

                    send(slot, 2, zz, side).start()
                    send(slot, 3, zz * B + y, core).start()

                return carry

            lax.fori_loop(0, 2, line, 0)

            def line_use(g, carry):
                zz = z + (2 * g - 1) * s

                @pl.when(valid(s, g, zz))
                def _():
                    consume(idx(zz, y, c))

                return carry

            lax.fori_loop(0, 2, line_use, 0)

            def across(g, carry):
                zz = z + (2 * g - 1) * (s - 1)

                @pl.when(valid(s - 1, g, zz))
                def _():
                    slot = idx(zz, 1 - y, c)
                    got(slot)
                    send(slot, 3, zz * B + 1 - y, core).start()
                    consume(slot)
                    slot2 = idx(zz, y, 1 - c)
                    got(slot2)
                    consume(slot2)

                return carry

            lax.fori_loop(0, 2, across, 0)

            def last(g, carry):
                zz = z + (2 * g - 1) * (s - 2)

                @pl.when(valid(s - 2, g, zz))
                def _():
                    slot = idx(zz, 1 - y, 1 - c)
                    got(slot)
                    consume(slot)

                return carry

            lax.fori_loop(0, 2, last, 0)
            return carry

        lax.fori_loop(1, A + 2, step, 0)

        def drain(zz, carry):
            slot = idx(zz, y, c)

            @pl.when((zz <= z) & (z < A - 1))
            def _():
                send(slot, 0, zz, above).wait_send()

            @pl.when((zz >= z) & (z > 0))
            def _():
                send(slot, 1, zz, below).wait_send()

            send(slot, 2, zz, side).wait_send()
            send(slot, 3, zz * B + y, core).wait_send()
            other = idx(zz, 1 - y, c)
            send(other, 3, zz * B + 1 - y, core).wait_send()
            return carry

        return lambda: lax.fori_loop(0, A, drain, 0)

    def project(slot):
        wide = X1[slot].astype(F32)
        ssq[...] += jnp.sum(wide * wide, axis=1, keepdims=True)
        piece = (wide * gain1_ref[slot]).astype(BF16)
        acc_q[...] += jnp.dot(piece, wq[slot], preferred_element_type=F32)
        acc_kv[...] += lax.dot_general(
            piece, wkv[slot], (((1,), (1,)), ((), ())), preferred_element_type=F32
        )

    def ready():
        q_load.wait()
        for j in range(n):
            kv_load(0, j).wait()
            kv_load(1, j).wait()
            wo_load(j).start()
        lm_load.start()

    drain1 = gather(X1, ag_s1, ag_r1, project, ready)

    scale = lax.rsqrt(ssq[...] / depth + 1e-05)
    kvs[...] = acc_kv[...] * scale
    piece_id, head_of = lax.rem(me, pieces), lax.div(me, pieces)

    def kv_send(i):
        return rc(kvs, kvr.at[piece_id], kv_s.at[i], kv_r.at[piece_id], head_of + KVH * i)

    for i in range(users):
        @pl.when(head_of + KVH * i != me)
        def _():
            kv_send(i).start()

        @pl.when(head_of + KVH * i == me)
        def _():
            kvr[piece_id] = kvs[...]

    cosine, sine = cos_ref[...], sin_ref[...]
    query = rope(acc_q[...] * scale, cosine, sine).astype(BF16)
    source = lax.rem(me, KVH) * pieces
    for i in range(pieces):
        @pl.when(source + i != me)
        def _():
            rc(kvs, kvr.at[i], kv_s.at[0], kv_r.at[i], core).wait_recv()

    key = jnp.concatenate([kvr[i, :, :kv_cols] for i in range(pieces)], axis=1)
    key = rope(key, cosine, sine).astype(BF16)
    value = jnp.concatenate([kvr[i, :, kv_cols:] for i in range(pieces)], axis=1).astype(BF16)
    seq_len = tokens // SEQS
    row = lax.broadcasted_iota(jnp.int32, (tokens, tokens), 0)
    col = lax.broadcasted_iota(jnp.int32, (tokens, tokens), 1)
    limit = jnp.full((tokens, tokens), len_ref[0], jnp.int32)
    for i in range(1, SEQS):
        limit = jnp.where(col >= i * seq_len, len_ref[i], limit)
    visible = (row // seq_len == col // seq_len) & (col <= row) & (col % seq_len < limit)
    scores = lax.dot_general(query, key, (((1,), (1,)), ((), ())), preferred_element_type=F32)
    scores = jnp.where(visible, scores / np.float32(np.sqrt(HD)), jnp.float32(-1e30))
    weights = jnp.exp(scores - jnp.max(scores, axis=1, keepdims=True))
    probs = (weights / jnp.sum(weights, axis=1, keepdims=True)).astype(BF16)
    attn[...] = jnp.dot(probs, value, preferred_element_type=F32).astype(BF16)
    for j in range(n):
        wo_load(j).wait()

    def partial(slot):
        return jnp.dot(attn[...], wo[slot], preferred_element_type=F32)

    def far_first(body):
        def step(i, carry):
            s = A - 1 - lax.div(i, 2)
            zz = z + (1 - 2 * lax.rem(i, 2)) * s

            @pl.when((zz >= 0) & (zz < A) & ((s > 0) | (lax.rem(i, 2) == 0)))
            def _():
                body(zz)

            return carry

        lax.fori_loop(0, 2 * A, step, 0)

    def core_copy(yy, zz):
        return rc(cs.at[yy, zz], cr.at[yy, zz], cs_s.at[yy, zz], cs_r.at[yy, zz], core)

    def to_core(yy):
        def body(zz):
            cs[yy, zz] = partial(idx(zz, yy, 1 - c)).astype(BF16)
            core_copy(yy, zz).start()

        return body

    def side_copy(zz):
        return rc(ys.at[zz], yr.at[zz], ys_s.at[zz], ys_r.at[zz], side)

    def to_side(zz):
        total = partial(idx(zz, 1 - y, c))
        core_copy(1 - y, zz).wait_recv()
        ys[zz] = (total + cr[1 - y, zz].astype(F32)).astype(BF16)
        side_copy(zz).start()

    def up_copy(zz):
        return rc(us.at[zz], ur.at[zz], us_s.at[zz], us_r.at[zz], above)

    def down_copy(zz):
        return rc(ds.at[zz], dr.at[zz], ds_s.at[zz], ds_r.at[zz], below)

    def both(zz):
        to_core(1 - y)(zz)

    far_first(both)
    far_first(to_side)
    far_first(lambda zz: to_core(y)(zz))

    def along(zz):
        total = partial(idx(zz, y, c))
        core_copy(y, zz).wait_recv()
        total += cr[y, zz].astype(F32)
        side_copy(zz).wait_recv()
        acc = total + yr[zz].astype(F32)

        @pl.when(zz > z)
        def _():
            @pl.when(z > 0)
            def _():
                up_copy(zz).wait_recv()
                us[zz] = (acc + ur[zz].astype(F32)).astype(BF16)

            @pl.when(z == 0)
            def _():
                us[zz] = acc.astype(BF16)

            up_copy(zz).start()

        @pl.when(zz < z)
        def _():
            @pl.when(z < A - 1)
            def _():
                down_copy(zz).wait_recv()
                ds[zz] = (acc + dr[zz].astype(F32)).astype(BF16)

            @pl.when(z == A - 1)
            def _():
                ds[zz] = acc.astype(BF16)

            down_copy(zz).start()

        @pl.when(zz == z)
        def _():
            tot[...] = acc

            @pl.when(z > 0)
            def _():
                up_copy(zz).wait_recv()
                tot[...] += ur[zz].astype(F32)

            @pl.when(z < A - 1)
            def _():
                down_copy(zz).wait_recv()
                tot[...] += dr[zz].astype(F32)

    far_first(along)
    layer = (x_ref[...].astype(F32) + tot[...]).astype(BF16)
    out_ref[...] = layer
    X2[me] = layer
    ssq[...] = jnp.zeros_like(ssq)

    def score(slot):
        wide = X2[slot].astype(F32)
        ssq[...] += jnp.sum(wide * wide, axis=1, keepdims=True)
        piece = (wide * gain2_ref[slot]).astype(BF16)
        acc_l[...] += jnp.dot(piece, lm[slot], preferred_element_type=F32)

    drain2 = gather(X2, ag_s2, ag_r2, score, lm_load.wait)

    logits = jnp.transpose(acc_l[...] * lax.rsqrt(ssq[...] / depth + 1e-05))
    vocab = logits.shape[0]
    word = lax.broadcasted_iota(jnp.int32, logits.shape, 0) + me * vocab
    picked = jnp.sum(jnp.where(word == ids_ref[...], logits, 0.0), axis=0, keepdims=True)
    top = jnp.max(logits, axis=0, keepdims=True)
    total = jnp.sum(jnp.exp(logits - top), axis=0, keepdims=True)
    st[me] = jnp.concatenate([top, total, picked, jnp.zeros((5, tokens), F32)], axis=0)

    def st_copy(slot, i, dev):
        return rc(st.at[slot], st.at[slot], st_s.at[i], st_r.at[slot], dev)

    def st_send(i, carry):
        st_copy(me, i, lax.rem(me + i, n)).start()
        return carry

    lax.fori_loop(1, n, st_send, 0)

    drain1()
    drain2()
    for i in range(users):
        @pl.when(head_of + KVH * i != me)
        def _():
            kv_send(i).wait_send()

    def rs_drain(zz, carry):
        core_copy(0, zz).wait_send()
        core_copy(1, zz).wait_send()
        side_copy(zz).wait_send()

        @pl.when(zz > z)
        def _():
            up_copy(zz).wait_send()

        @pl.when(zz < z)
        def _():
            down_copy(zz).wait_send()

        return carry

    lax.fori_loop(0, A, rs_drain, 0)

    def st_got(i, carry):
        slot = lax.rem(me + i, n)
        st_copy(slot, i, core).wait_recv()
        st_copy(me, i, slot).wait_send()
        return carry

    lax.fori_loop(1, n, st_got, 0)
    parts = st[...]
    tops, totals, hits = parts[:, 0, :], parts[:, 1, :], parts[:, 2, :]
    peak = jnp.max(tops, axis=0, keepdims=True)
    whole = jnp.sum(totals * jnp.exp(tops - peak), axis=0, keepdims=True)
    logp_ref[...] = jnp.sum(hits, axis=0, keepdims=True) - peak - jnp.log(whole)


def body(
    stream, target_ids, lengths, attn_gain, w_query, w_key, w_value, w_out, final_gain, lm_head
):
    tokens, width = stream.shape
    depth = w_query.shape[0]
    n = depth // width
    A = n // (B * C)
    kv_cols, vocab = w_key.shape[1], lm_head.shape[1]
    users, pieces = n // KVH, HD // kv_cols
    cosine, sine = rope_tables(tokens)
    across = [w_key.T, w_value.T, w_out]
    if width % 128:
        across = [w.reshape(-1, n, width).transpose(1, 0, 2) for w in across]
    wk_t, wv_t, w_out = across
    vmem = pl.BlockSpec(memory_space=pltpu.VMEM)
    smem = pl.BlockSpec(memory_space=pltpu.SMEM)
    hbm = pl.BlockSpec(memory_space=pl.ANY)
    block = (tokens, width)
    dma = pltpu.SemaphoreType.DMA
    V = pltpu.VMEM
    layer_out, logp = pl.pallas_call(
        functools.partial(kernel, n, depth),
        out_shape=(
            jax.ShapeDtypeStruct(block, BF16),
            jax.ShapeDtypeStruct((1, tokens), F32),
        ),
        in_specs=[vmem, vmem, smem] + [vmem] * 4 + [hbm] * 5,
        out_specs=(vmem, vmem),
        scratch_shapes=[
            V((n, width, HD), BF16), V((n, 2 * kv_cols, width), BF16),
            V((n, HD, width), BF16), V((n, width, vocab), BF16),
            V((n,) + block, BF16), V((n,) + block, BF16),
            V((tokens, HD), F32), V((tokens, 2 * kv_cols), F32),
            V((tokens, 1), F32), V((tokens, vocab), F32),
            V((tokens, 2 * kv_cols), F32), V((pieces, tokens, 2 * kv_cols), F32),
            V((tokens, HD), BF16),
            V((2, A) + block, BF16), V((2, A) + block, BF16),
            V((A,) + block, BF16), V((A,) + block, BF16),
            V((A,) + block, BF16), V((A,) + block, BF16),
            V((A,) + block, BF16), V((A,) + block, BF16),
            V(block, F32), V((n, 8, tokens), F32),
            dma((2,)), dma((2, n)), dma((n,)),
            dma((4, B * A)), dma((n,)), dma((4, B * A)), dma((n,)),
            dma((users,)), dma((pieces,)),
            dma((2, A)), dma((2, A)), dma((A,)), dma((A,)),
            dma((A,)), dma((A,)), dma((A,)), dma((A,)),
            dma((n,)), dma((n,)),
        ],
        compiler_params=pltpu.CompilerParams(
            collective_id=0, has_side_effects=True, vmem_limit_bytes=56 * 1024 * 1024
        ),
        cost_estimate=pl.CostEstimate(
            flops=2 * tokens * depth * (2 * HD + 2 * kv_cols + vocab),
            bytes_accessed=2 * depth * (2 * HD + 2 * kv_cols + vocab),
            transcendentals=0,
        ),
    )(
        stream, target_ids.reshape(1, tokens), lengths,
        attn_gain.reshape(n, 1, width), final_gain.reshape(n, 1, width),
        jnp.asarray(cosine), jnp.asarray(sine),
        w_query.reshape(n, width, HD), wk_t, wv_t, w_out, lm_head.reshape(n, width, vocab),
    )
    return layer_out, logp.reshape(tokens)


def solution(mesh):
    return jax.shard_map(
        body,
        mesh=mesh,
        in_specs=(
            P("groups", "mp"),
            P("groups"),
            P("groups"),
            P(),
            P(None, "mp"),
            P(None, "mp"),
            P(None, "mp"),
            P("mp", None),
            P(),
            P(None, "mp"),
        ),
        out_specs=(P("groups", "mp"), P("groups")),
        check_vma=False,
    )
```

```python
import functools

import jax
import jax.numpy as jnp
import numpy as np
from jax import lax
from jax.experimental import pallas as pl
from jax.experimental.pallas import tpu as pltpu
from jax.sharding import PartitionSpec as P

KVH = 8
HD = 128
SEQS = 2
B, C = 2, 2
HALVES = 2
BF16, F32 = jnp.bfloat16, jnp.float32


def rope_tables(tokens):
    positions = (np.arange(tokens) % (tokens // SEQS)).astype(np.float32)
    within = 2 * (np.arange(HD) // 2)
    freq = np.power(np.float32(1000000.0), -within.astype(np.float32) / np.float32(HD))
    angle = (positions[:, None] * freq[None, :].astype(np.float32)).astype(np.float32)
    sine = np.sin(angle.astype(np.float64))
    sine = np.where(np.arange(HD)[None, :] % 2 == 0, -sine, sine)
    return np.cos(angle.astype(np.float64)).astype(np.float32), sine.astype(np.float32)


def rope(values, cosine, sine):
    even = lax.broadcasted_iota(jnp.int32, values.shape, 1) % 2 == 0
    swapped = jnp.where(even, pltpu.roll(values, HD - 1, 1), pltpu.roll(values, 1, 1))
    return values * cosine + swapped * sine


def kernel(
    n, depth,
    x_ref, ids_ref, len_ref, gain1_ref, gain2_ref, cos_ref, sin_ref,
    wq_hbm, wk_hbm, wv_hbm, wo_hbm, lm_hbm,
    out_ref, logp_ref,
    wq, wkv, wo, lm, X1, X2, acc_q, acc_kv, ssq, acc_l,
    kvs, kvr, attn, cs, cr, ys, yr, us, ur, ds, dr, tot, st,
    wsem, wkvsem, wosem, ag_s1, ag_r1, ag_s2, ag_r2, kv_s, kv_r,
    cs_s, cs_r, ys_s, ys_r, us_s, us_r, ds_s, ds_r, st_s, st_r,
):
    A = n // (B * C)
    me = lax.axis_index("mp")
    c = lax.rem(me, C)
    y = lax.rem(lax.div(me, C), B)
    z = lax.div(me, B * C)
    tokens, width = x_ref.shape
    kv_cols = wkv.shape[1] // 2
    pieces = HD // kv_cols
    users = n // KVH

    def idx(zz, yy, cc):
        return (zz * B + yy) * C + cc

    core, side = idx(z, y, 1 - c), idx(z, 1 - y, c)
    above, below = idx(z + 1, y, c), idx(z - 1, y, c)

    def rc(src, dst, ssem, rsem, dev):
        return pltpu.make_async_remote_copy(
            src_ref=src, dst_ref=dst, send_sem=ssem, recv_sem=rsem,
            device_id={"mp": dev}, device_id_type=pl.DeviceIdType.MESH,
        )

    def columns(ref, j):
        return ref.at[j] if len(ref.shape) == 3 else ref.at[:, j * width:(j + 1) * width]

    q_load = pltpu.make_async_copy(wq_hbm, wq, wsem.at[0])
    lm_load = pltpu.make_async_copy(lm_hbm, lm, wsem.at[1])

    def kv_load(i, j):
        return pltpu.make_async_copy(
            columns((wk_hbm, wv_hbm)[i], j),
            wkv.at[j, i * kv_cols:(i + 1) * kv_cols],
            wkvsem.at[i, j],
        )

    def wo_load(j):
        return pltpu.make_async_copy(columns(wo_hbm, j), wo.at[j], wosem.at[j])

    barrier = pltpu.get_barrier_semaphore()

    def greet(i, carry):
        pl.semaphore_signal(
            barrier, inc=1, device_id={"mp": lax.rem(me + i, n)}, device_id_type=pl.DeviceIdType.MESH
        )
        return carry

    lax.fori_loop(1, n, greet, 0)
    q_load.start()
    for j in range(n):
        kv_load(0, j).start()
        kv_load(1, j).start()
    X1[me] = x_ref[...]
    acc_q[...] = jnp.zeros_like(acc_q)
    acc_kv[...] = jnp.zeros_like(acc_kv)
    acc_l[...] = jnp.zeros_like(acc_l)
    ssq[...] = jnp.zeros_like(ssq)
    pl.semaphore_wait(barrier, n - 1)

    def gather(X, ss, rs, consume, prepare):
        rows = tokens // HALVES

        def send(slot, kind, k, dev, h):
            view = X.at[slot, h * rows:(h + 1) * rows]
            return rc(view, view, ss.at[h, kind, k], rs.at[h, slot], dev)

        def got(slot, h):
            send(slot, 0, 0, core, h).wait_recv()

        for h in range(HALVES):
            @pl.when(z < A - 1)
            def _():
                send(me, 0, z, above, h).start()

            @pl.when(z > 0)
            def _():
                send(me, 1, z, below, h).start()

            send(me, 2, z, side, h).start()
        for h in range(HALVES):
            send(me, 3, z * B + y, core, h).start()
        prepare()
        consume(me)

        def valid(k, g, zz):
            return (k >= 0) & (k < A) & (zz >= 0) & (zz < A) & ((k > 0) | (g == 0))

        def step(s, carry):
            def line(g, carry):
                zz = z + (2 * g - 1) * s

                @pl.when(valid(s, g, zz))
                def _():
                    slot = idx(zz, y, c)
                    for h in range(HALVES):
                        got(slot, h)

                        @pl.when((g == 0) & (z < A - 1))
                        def _():
                            send(slot, 0, zz, above, h).start()

                        @pl.when((g == 1) & (z > 0))
                        def _():
                            send(slot, 1, zz, below, h).start()

                        send(slot, 2, zz, side, h).start()
                        send(slot, 3, zz * B + y, core, h).start()

                return carry

            lax.fori_loop(0, 2, line, 0)

            def line_use(g, carry):
                zz = z + (2 * g - 1) * s

                @pl.when(valid(s, g, zz))
                def _():
                    consume(idx(zz, y, c))

                return carry

            lax.fori_loop(0, 2, line_use, 0)

            def across(g, carry):
                zz = z + (2 * g - 1) * (s - 1)

                @pl.when(valid(s - 1, g, zz))
                def _():
                    slot = idx(zz, 1 - y, c)
                    for h in range(HALVES):
                        got(slot, h)
                        send(slot, 3, zz * B + 1 - y, core, h).start()
                    consume(slot)
                    slot2 = idx(zz, y, 1 - c)
                    for h in range(HALVES):
                        got(slot2, h)
                    consume(slot2)

                return carry

            lax.fori_loop(0, 2, across, 0)

            def last(g, carry):
                zz = z + (2 * g - 1) * (s - 2)

                @pl.when(valid(s - 2, g, zz))
                def _():
                    slot = idx(zz, 1 - y, 1 - c)
                    for h in range(HALVES):
                        got(slot, h)
                    consume(slot)

                return carry

            lax.fori_loop(0, 2, last, 0)
            return carry

        lax.fori_loop(1, A + 2, step, 0)

        def drain(zz, carry):
            slot = idx(zz, y, c)

            other = idx(zz, 1 - y, c)
            for h in range(HALVES):
                @pl.when((zz <= z) & (z < A - 1))
                def _():
                    send(slot, 0, zz, above, h).wait_send()

                @pl.when((zz >= z) & (z > 0))
                def _():
                    send(slot, 1, zz, below, h).wait_send()

                send(slot, 2, zz, side, h).wait_send()
                send(slot, 3, zz * B + y, core, h).wait_send()
                send(other, 3, zz * B + 1 - y, core, h).wait_send()
            return carry

        return lambda: lax.fori_loop(0, A, drain, 0)

    def project(slot):
        wide = X1[slot].astype(F32)
        ssq[...] += jnp.sum(wide * wide, axis=1, keepdims=True)
        piece = (wide * gain1_ref[slot]).astype(BF16)
        acc_q[...] += jnp.dot(piece, wq[slot], preferred_element_type=F32)
        acc_kv[...] += lax.dot_general(
            piece, wkv[slot], (((1,), (1,)), ((), ())), preferred_element_type=F32
        )

    def ready():
        q_load.wait()
        for j in range(n):
            kv_load(0, j).wait()
            kv_load(1, j).wait()
            wo_load(j).start()
        lm_load.start()

    drain1 = gather(X1, ag_s1, ag_r1, project, ready)

    scale = lax.rsqrt(ssq[...] / depth + 1e-05)
    kvs[...] = acc_kv[...] * scale
    piece_id, head_of = lax.rem(me, pieces), lax.div(me, pieces)

    def kv_send(i):
        return rc(kvs, kvr.at[piece_id], kv_s.at[i], kv_r.at[piece_id], head_of + KVH * i)

    for i in range(users):
        @pl.when(head_of + KVH * i != me)
        def _():
            kv_send(i).start()

        @pl.when(head_of + KVH * i == me)
        def _():
            kvr[piece_id] = kvs[...]

    cosine, sine = cos_ref[...], sin_ref[...]
    query = rope(acc_q[...] * scale, cosine, sine).astype(BF16)
    source = lax.rem(me, KVH) * pieces
    for i in range(pieces):
        @pl.when(source + i != me)
        def _():
            rc(kvs, kvr.at[i], kv_s.at[0], kv_r.at[i], core).wait_recv()

    key = jnp.concatenate([kvr[i, :, :kv_cols] for i in range(pieces)], axis=1)
    key = rope(key, cosine, sine).astype(BF16)
    value = jnp.concatenate([kvr[i, :, kv_cols:] for i in range(pieces)], axis=1).astype(BF16)
    seq_len = tokens // SEQS
    row = lax.broadcasted_iota(jnp.int32, (tokens, tokens), 0)
    col = lax.broadcasted_iota(jnp.int32, (tokens, tokens), 1)
    limit = jnp.full((tokens, tokens), len_ref[0], jnp.int32)
    for i in range(1, SEQS):
        limit = jnp.where(col >= i * seq_len, len_ref[i], limit)
    visible = (row // seq_len == col // seq_len) & (col <= row) & (col % seq_len < limit)
    scores = lax.dot_general(query, key, (((1,), (1,)), ((), ())), preferred_element_type=F32)
    scores = jnp.where(visible, scores / np.float32(np.sqrt(HD)), jnp.float32(-1e30))
    weights = jnp.exp(scores - jnp.max(scores, axis=1, keepdims=True))
    probs = (weights / jnp.sum(weights, axis=1, keepdims=True)).astype(BF16)
    attn[...] = jnp.dot(probs, value, preferred_element_type=F32).astype(BF16)
    for j in range(n):
        wo_load(j).wait()

    def partial(slot):
        return jnp.dot(attn[...], wo[slot], preferred_element_type=F32)

    def far_first(body):
        def step(i, carry):
            s = A - 1 - lax.div(i, 2)
            zz = z + (1 - 2 * lax.rem(i, 2)) * s

            @pl.when((zz >= 0) & (zz < A) & ((s > 0) | (lax.rem(i, 2) == 0)))
            def _():
                body(zz)

            return carry

        lax.fori_loop(0, 2 * A, step, 0)

    def core_copy(yy, zz):
        return rc(cs.at[yy, zz], cr.at[yy, zz], cs_s.at[yy, zz], cs_r.at[yy, zz], core)

    def to_core(yy):
        def body(zz):
            cs[yy, zz] = partial(idx(zz, yy, 1 - c)).astype(BF16)
            core_copy(yy, zz).start()

        return body

    def side_copy(zz):
        return rc(ys.at[zz], yr.at[zz], ys_s.at[zz], ys_r.at[zz], side)

    def to_side(zz):
        total = partial(idx(zz, 1 - y, c))
        core_copy(1 - y, zz).wait_recv()
        ys[zz] = (total + cr[1 - y, zz].astype(F32)).astype(BF16)
        side_copy(zz).start()

    def up_copy(zz):
        return rc(us.at[zz], ur.at[zz], us_s.at[zz], us_r.at[zz], above)

    def down_copy(zz):
        return rc(ds.at[zz], dr.at[zz], ds_s.at[zz], ds_r.at[zz], below)

    def both(zz):
        to_core(1 - y)(zz)

    far_first(both)
    far_first(to_side)
    far_first(lambda zz: to_core(y)(zz))

    def along(zz):
        total = partial(idx(zz, y, c))
        core_copy(y, zz).wait_recv()
        total += cr[y, zz].astype(F32)
        side_copy(zz).wait_recv()
        acc = total + yr[zz].astype(F32)

        @pl.when(zz > z)
        def _():
            @pl.when(z > 0)
            def _():
                up_copy(zz).wait_recv()
                us[zz] = (acc + ur[zz].astype(F32)).astype(BF16)

            @pl.when(z == 0)
            def _():
                us[zz] = acc.astype(BF16)

            up_copy(zz).start()

        @pl.when(zz < z)
        def _():
            @pl.when(z < A - 1)
            def _():
                down_copy(zz).wait_recv()
                ds[zz] = (acc + dr[zz].astype(F32)).astype(BF16)

            @pl.when(z == A - 1)
            def _():
                ds[zz] = acc.astype(BF16)

            down_copy(zz).start()

        @pl.when(zz == z)
        def _():
            tot[...] = acc

            @pl.when(z > 0)
            def _():
                up_copy(zz).wait_recv()
                tot[...] += ur[zz].astype(F32)

            @pl.when(z < A - 1)
            def _():
                down_copy(zz).wait_recv()
                tot[...] += dr[zz].astype(F32)

    far_first(along)
    layer = (x_ref[...].astype(F32) + tot[...]).astype(BF16)
    out_ref[...] = layer
    X2[me] = layer
    ssq[...] = jnp.zeros_like(ssq)

    def score(slot):
        wide = X2[slot].astype(F32)
        ssq[...] += jnp.sum(wide * wide, axis=1, keepdims=True)
        piece = (wide * gain2_ref[slot]).astype(BF16)
        acc_l[...] += jnp.dot(piece, lm[slot], preferred_element_type=F32)

    drain2 = gather(X2, ag_s2, ag_r2, score, lm_load.wait)

    logits = jnp.transpose(acc_l[...] * lax.rsqrt(ssq[...] / depth + 1e-05))
    vocab = logits.shape[0]
    word = lax.broadcasted_iota(jnp.int32, logits.shape, 0) + me * vocab
    picked = jnp.sum(jnp.where(word == ids_ref[...], logits, 0.0), axis=0, keepdims=True)
    top = jnp.max(logits, axis=0, keepdims=True)
    total = jnp.sum(jnp.exp(logits - top), axis=0, keepdims=True)
    st[me] = jnp.concatenate([top, total, picked, jnp.zeros((5, tokens), F32)], axis=0)

    def st_copy(slot, i, dev):
        return rc(st.at[slot], st.at[slot], st_s.at[i], st_r.at[slot], dev)

    def st_send(i, carry):
        st_copy(me, i, lax.rem(me + i, n)).start()
        return carry

    lax.fori_loop(1, n, st_send, 0)

    drain1()
    drain2()
    for i in range(users):
        @pl.when(head_of + KVH * i != me)
        def _():
            kv_send(i).wait_send()

    def rs_drain(zz, carry):
        core_copy(0, zz).wait_send()
        core_copy(1, zz).wait_send()
        side_copy(zz).wait_send()

        @pl.when(zz > z)
        def _():
            up_copy(zz).wait_send()

        @pl.when(zz < z)
        def _():
            down_copy(zz).wait_send()

        return carry

    lax.fori_loop(0, A, rs_drain, 0)

    def st_got(i, carry):
        slot = lax.rem(me + i, n)
        st_copy(slot, i, core).wait_recv()
        st_copy(me, i, slot).wait_send()
        return carry

    lax.fori_loop(1, n, st_got, 0)
    parts = st[...]
    tops, totals, hits = parts[:, 0, :], parts[:, 1, :], parts[:, 2, :]
    peak = jnp.max(tops, axis=0, keepdims=True)
    whole = jnp.sum(totals * jnp.exp(tops - peak), axis=0, keepdims=True)
    logp_ref[...] = jnp.sum(hits, axis=0, keepdims=True) - peak - jnp.log(whole)


def body(
    stream, target_ids, lengths, attn_gain, w_query, w_key, w_value, w_out, final_gain, lm_head
):
    tokens, width = stream.shape
    depth = w_query.shape[0]
    n = depth // width
    A = n // (B * C)
    kv_cols, vocab = w_key.shape[1], lm_head.shape[1]
    users, pieces = n // KVH, HD // kv_cols
    cosine, sine = rope_tables(tokens)
    across = [w_key.T, w_value.T, w_out]
    if width % 128:
        across = [w.reshape(-1, n, width).transpose(1, 0, 2) for w in across]
    wk_t, wv_t, w_out = across
    vmem = pl.BlockSpec(memory_space=pltpu.VMEM)
    smem = pl.BlockSpec(memory_space=pltpu.SMEM)
    hbm = pl.BlockSpec(memory_space=pl.ANY)
    block = (tokens, width)
    dma = pltpu.SemaphoreType.DMA
    V = pltpu.VMEM
    layer_out, logp = pl.pallas_call(
        functools.partial(kernel, n, depth),
        out_shape=(
            jax.ShapeDtypeStruct(block, BF16),
            jax.ShapeDtypeStruct((1, tokens), F32),
        ),
        in_specs=[vmem, vmem, smem] + [vmem] * 4 + [hbm] * 5,
        out_specs=(vmem, vmem),
        scratch_shapes=[
            V((n, width, HD), BF16), V((n, 2 * kv_cols, width), BF16),
            V((n, HD, width), BF16), V((n, width, vocab), BF16),
            V((n,) + block, BF16), V((n,) + block, BF16),
            V((tokens, HD), F32), V((tokens, 2 * kv_cols), F32),
            V((tokens, 1), F32), V((tokens, vocab), F32),
            V((tokens, 2 * kv_cols), F32), V((pieces, tokens, 2 * kv_cols), F32),
            V((tokens, HD), BF16),
            V((2, A) + block, BF16), V((2, A) + block, BF16),
            V((A,) + block, BF16), V((A,) + block, BF16),
            V((A,) + block, BF16), V((A,) + block, BF16),
            V((A,) + block, BF16), V((A,) + block, BF16),
            V(block, F32), V((n, 8, tokens), F32),
            dma((2,)), dma((2, n)), dma((n,)),
            dma((HALVES, 4, B * A)), dma((HALVES, n)), dma((HALVES, 4, B * A)), dma((HALVES, n)),
            dma((users,)), dma((pieces,)),
            dma((2, A)), dma((2, A)), dma((A,)), dma((A,)),
            dma((A,)), dma((A,)), dma((A,)), dma((A,)),
            dma((n,)), dma((n,)),
        ],
        compiler_params=pltpu.CompilerParams(
            collective_id=0, has_side_effects=True, vmem_limit_bytes=56 * 1024 * 1024
        ),
        cost_estimate=pl.CostEstimate(
            flops=2 * tokens * depth * (2 * HD + 2 * kv_cols + vocab),
            bytes_accessed=2 * depth * (2 * HD + 2 * kv_cols + vocab),
            transcendentals=0,
        ),
    )(
        stream, target_ids.reshape(1, tokens), lengths,
        attn_gain.reshape(n, 1, width), final_gain.reshape(n, 1, width),
        jnp.asarray(cosine), jnp.asarray(sine),
        w_query.reshape(n, width, HD), wk_t, wv_t, w_out, lm_head.reshape(n, width, vocab),
    )
    return layer_out, logp.reshape(tokens)


def solution(mesh):
    return jax.shard_map(
        body,
        mesh=mesh,
        in_specs=(
            P("groups", "mp"),
            P("groups"),
            P("groups"),
            P(),
            P(None, "mp"),
            P(None, "mp"),
            P(None, "mp"),
            P("mp", None),
            P(),
            P(None, "mp"),
        ),
        out_specs=(P("groups", "mp"), P("groups")),
        check_vma=False,
    )
```
